32 devices in a mesh: ctx: 8 (over z, x), tp: 4 (over y, core).
Axes of the slice: x: 2, y: 2, z: 4, core: 2. Of those that a mesh axis runs over, the one named last changes fastest.
Arguments:
- query_rows: bfloat16 [2048, 4096], P('ctx', 'tp'), may hold values from -6 to 6
- key_rows: bfloat16 [2048, 4096], P('ctx', 'tp'), may hold values from -6 to 6
- value_rows: bfloat16 [2048, 4096], P('ctx', 'tp'), may hold values from -6 to 6
- filters: bfloat16 [2048, 4096], P('ctx', 'tp'), may hold values from -1 to 1
- skip_gain: float32 [4096], P('tp'), may hold values from 0.5 to 1.5
- out_weight: bfloat16 [4096, 4096], P('tp', 'ctx'), may hold values from -0.125 to 0.125
Outputs:
- mixed_out: bfloat16 [2048, 4096], P('ctx', 'tp')
The draws below stay inside these ranges and needn't reach their ends.
All inputs are finite; a program needn't handle non-finite values.
Results may differ from the reference program's by a relative error of at most 0.0057.
Values may be sent and summed in bfloat16 or wider, within the bound.
A program may use at most 128 MiB of HBM per device.

```python
import jax
import jax.numpy as jnp
from jax import lax

MIXER_WIDTH = 4096
TOKEN_COUNT = 2048


def draw_filters(key, part):
    key = jax.random.fold_in(key, 11)
    jitter_seed_stream, damping_seed_stream, impulse_seed_stream = jax.random.split(key, 3)
    kernel_offsets = jnp.arange(TOKEN_COUNT, dtype=jnp.float32)[:, None]
    rates = jnp.exp(jax.random.uniform(damping_seed_stream, (MIXER_WIDTH,), jnp.float32, jnp.log(0.5), jnp.log(TOKEN_COUNT / 40.0)))
    noise = jax.random.truncated_normal(jitter_seed_stream, -4.0, 4.0, (TOKEN_COUNT, MIXER_WIDTH), jnp.float32)
    sparse_impulses = jax.random.randint(impulse_seed_stream, (3, MIXER_WIDTH), 0, TOKEN_COUNT).astype(jnp.float32)
    exponential_envelope = jnp.ones((TOKEN_COUNT, MIXER_WIDTH), jnp.float32)
    for offset_position in range(3):
        exponential_envelope = exponential_envelope * jnp.where(kernel_offsets >= sparse_impulses[offset_position][None, :], 0.6, 1.0)
    envelope = jnp.exp(-rates[None, :] * kernel_offsets / TOKEN_COUNT)
    energy = (1.0 - jnp.exp(-2.0 * rates)) / (1.0 - jnp.exp(-2.0 * rates / TOKEN_COUNT))
    values = noise * envelope * exponential_envelope / jnp.sqrt(energy)[None, :]
    return values.astype(jnp.bfloat16)


def spiked(result, key, source, target, parts, factor):
    def block_of(dim):
        return (jnp.arange(result.shape[dim]) // (result.shape[dim] // parts)).reshape((-1,) + (1,) * (result.ndim - 1 - dim))

    first = jax.random.permutation(key, parts)[block_of(target)]
    second = (block_of(target) + parts // 2) % parts
    return jnp.where((block_of(source) == first) | (block_of(source) == second), factor * result, result)


def block_levels(own_key, dims, cuts, least, top_value):
    def one(dim, shards_of):
        heights = jax.random.uniform(jax.random.fold_in(jax.random.fold_in(own_key, 6), dim), (shards_of,), jnp.float32, least / len(cuts), top_value / len(cuts))
        return jnp.repeat(jnp.exp(heights), dims[dim] // shards_of).reshape((-1,) + (1,) * (len(dims) - dim - 1))

    gain = one(*cuts[0])
    for cut in cuts[1:]:
        gain = gain * one(*cut)
    return gain


def gaussian(rng, extent, scale, most, pieces=(), kind=jnp.bfloat16):
    loudness = block_levels(rng, extent, pieces, -0.22, 0.18) if pieces else 1.0
    array = jax.random.normal(rng, extent, jnp.float32) * scale * loudness
    return jnp.minimum(jnp.maximum(array, -most), most).astype(kind)


def bell_draw_with(stream_key, extent, scale, most, pieces, heavy, held_as=jnp.bfloat16):
    drawn = scale * jax.random.normal(stream_key, extent, jnp.float32)
    if pieces:
        drawn = drawn * block_levels(stream_key, extent, pieces, -0.22, 0.18)
    return jnp.clip(spiked(drawn, jax.random.fold_in(stream_key, 3), *heavy), -most, most).astype(held_as)


def setup_inputs(seed: int = 0) -> dict:
    streams_of = jax.random.split(jax.random.key(seed), 7)
    query_rows = gaussian(streams_of[0], (TOKEN_COUNT, MIXER_WIDTH), 1.0, 6.0, ((0, 8), (1, 4)))
    key_rows = gaussian(streams_of[1], (TOKEN_COUNT, MIXER_WIDTH), 1.0, 6.0, ((0, 8), (1, 4)))
    value_rows = gaussian(streams_of[2], (TOKEN_COUNT, MIXER_WIDTH), 1.0, 6.0, ((0, 8), (1, 4)))
    filters = draw_filters(jax.random.fold_in(streams_of[6], 71), 0)
    skip_gain = jnp.clip(0.5 + 1.0 * jax.random.uniform(streams_of[4], (MIXER_WIDTH,), jnp.float32) ** block_levels(streams_of[4], (MIXER_WIDTH,), ((0, 4),), -0.2, 0.2), 0.5, 1.5)
    out_weight = bell_draw_with(streams_of[5], (MIXER_WIDTH, MIXER_WIDTH), MIXER_WIDTH ** -0.5, 0.125, ((0, 4), (1, 8)), (0, 1, 8, 2.0))
    return dict(query_rows=query_rows, key_rows=key_rows, value_rows=value_rows, filters=filters, skip_gain=skip_gain, out_weight=out_weight)


def reference(query_rows, key_rows, value_rows, filters, skip_gain, out_weight):
    mixed_in = (key_rows.astype(jnp.float32) * value_rows.astype(jnp.float32)).astype(jnp.bfloat16)
    length = mixed_in.shape[0]
    model_width = mixed_in.shape[1]
    block_size = min(model_width, 256)
    blocks = model_width // block_size
    signal = mixed_in.astype(jnp.float32).reshape(length, blocks, block_size).transpose(1, 0, 2)
    kernel = filters.astype(jnp.float32).reshape(length, blocks, block_size).transpose(1, 0, 2)

    def convolve(pair):
        series, taps = pair
        spectrum = jnp.fft.rfft(series, n=2 * length, axis=0) * jnp.fft.rfft(taps, n=2 * length, axis=0)
        return jnp.fft.irfft(spectrum, n=2 * length, axis=0)[:length].astype(jnp.float32)

    convolved = lax.map(convolve, (signal, kernel)).transpose(1, 0, 2).reshape(length, model_width)
    gated_rows = (query_rows.astype(jnp.float32) * (convolved + skip_gain[None, :] * mixed_in.astype(jnp.float32))).astype(jnp.bfloat16)
    return jnp.dot(gated_rows, out_weight, preferred_element_type=jnp.float32).astype(jnp.bfloat16)
```

```python
import functools
import math

import jax
import jax.numpy as jnp
import ml_dtypes
import numpy as np
from jax import lax
from jax.experimental import pallas as pl
from jax.experimental.pallas import tpu as pltpu
from jax.sharding import PartitionSpec as P

precise = lax.Precision.HIGHEST
MESH = pl.DeviceIdType.MESH
LANES = 128
INNER = 8
f32 = jnp.float32
bf16 = jnp.bfloat16


def make_tables(full_len, size_one, second):
    index_one = jnp.arange(size_one, dtype=jnp.int32)
    half_one = jnp.arange(size_one // 2, dtype=jnp.int32)
    index_two = jnp.arange(second, dtype=jnp.int32)
    angle_one = (
        2.0
        * math.pi
        / size_one
        * (index_one[:, None] * half_one[None, :] % size_one).astype(jnp.float32)
    )
    angle_two = (
        2.0
        * math.pi
        / second
        * (index_two[:, None] * index_two[None, :] % second).astype(jnp.float32)
    )
    angle_mid = (
        2.0
        * math.pi
        / full_len
        * (index_one[:, None] * index_two[None, :] % full_len).astype(jnp.float32)
    )
    return (
        jnp.cos(angle_one),
        jnp.sin(angle_one),
        jnp.cos(angle_two),
        jnp.sin(angle_two),
        jnp.cos(angle_mid),
        jnp.sin(angle_mid),
    )


def along_second(matrix, table):
    return jnp.einsum("mkb,bj->mkj", matrix, table, precision=precise)


def forward_spectrum(signal, tables, size_one, second):
    cos_one, sin_one, cos_two, sin_two, cos_mid, sin_mid = tables
    reshaped = signal.reshape(signal.shape[0], size_one // 2, second)
    real_a = jnp.einsum("ka,mab->mkb", cos_one, reshaped, precision=precise)
    imag_a = -jnp.einsum("ka,mab->mkb", sin_one, reshaped, precision=precise)
    real_b = real_a * cos_mid + imag_a * sin_mid
    imag_b = imag_a * cos_mid - real_a * sin_mid
    real_c = along_second(real_b, cos_two) + along_second(imag_b, sin_two)
    imag_c = along_second(imag_b, cos_two) - along_second(real_b, sin_two)
    return (real_c, imag_c)


def inverse_signal(real_p, imag_p, tables, full_len):
    cos_one, sin_one, cos_two, sin_two, cos_mid, sin_mid = tables
    real_q = along_second(real_p, cos_two) - along_second(imag_p, sin_two)
    imag_q = along_second(imag_p, cos_two) + along_second(real_p, sin_two)
    real_r = real_q * cos_mid - imag_q * sin_mid
    imag_r = real_q * sin_mid + imag_q * cos_mid
    result = jnp.einsum("ka,mkb->mab", cos_one, real_r, precision=precise) - jnp.einsum(
        "ka,mkb->mab", sin_one, imag_r, precision=precise
    )
    return (result / full_len).reshape(real_p.shape[0], full_len // 2)


def convolve_block(series, taps):
    length = series.shape[-1]
    full_len = 2 * length
    size_one = 1 << (full_len.bit_length() - 1) // 2
    second = full_len // size_one
    tables = make_tables(full_len, size_one, second)
    channels = series.shape[0]
    stacked = jnp.concatenate([series.astype(jnp.float32), taps.astype(jnp.float32)], axis=0)
    real_s, imag_s = forward_spectrum(stacked, tables, size_one, second)
    real_u, real_h = (real_s[:channels], real_s[channels:])
    imag_u, imag_h = (imag_s[:channels], imag_s[channels:])
    real_p = real_u * real_h - imag_u * imag_h
    imag_p = real_u * imag_h + imag_u * real_h
    return inverse_signal(real_p, imag_p, tables, full_len)


def plain_path(query_rows, key_rows, value_rows, filters, skip_gain, out_weight):
    row_count, chan_count = key_rows.shape
    groups = lax.axis_size("ctx")
    per_group = chan_count // groups
    mixed_in = (key_rows.astype(jnp.float32) * value_rows.astype(jnp.float32)).astype(jnp.bfloat16)
    series_t = mixed_in.T.reshape(groups, per_group, row_count)
    taps_t = filters.T.reshape(groups, per_group, row_count)
    series_p = lax.all_to_all(series_t, "ctx", split_axis=0, concat_axis=2, tiled=True)
    taps_p = lax.all_to_all(taps_t, "ctx", split_axis=0, concat_axis=2, tiled=True)
    result = convolve_block(series_p[0], taps_p[0])[None]
    returned = lax.all_to_all(result, "ctx", split_axis=2, concat_axis=0, tiled=True)
    convolved = returned.reshape(chan_count, row_count).T
    gated_rows = (
        query_rows.astype(jnp.float32)
        * (convolved + skip_gain[None, :] * mixed_in.astype(jnp.float32))
    ).astype(jnp.bfloat16)
    partial_value = jnp.dot(
        gated_rows,
        lax.all_gather(out_weight, "ctx", axis=1, tiled=True),
        preferred_element_type=jnp.float32,
    )
    return lax.psum_scatter(partial_value, "tp", scatter_dimension=1, tiled=True).astype(
        jnp.bfloat16
    )


def split_table(table):
    high = table.astype(ml_dtypes.bfloat16)
    low = (table - high.astype(np.float64)).astype(ml_dtypes.bfloat16)
    return high, low


def block_tables(blocks):
    angle = np.pi * (np.arange(blocks) + 0.5) / blocks
    phase = np.outer(angle, np.arange(blocks))
    forward = np.concatenate([np.cos(phase), -np.sin(phase)], axis=0)
    inverse = np.concatenate([np.cos(phase.T), -np.sin(phase.T)], axis=1) / blocks
    forward_high, forward_low = split_table(forward)
    inverse_high, inverse_low = split_table(inverse)
    twist = np.stack([np.cos(angle), -np.sin(angle)])[:, :, None]
    twist = np.broadcast_to(twist, (2, blocks, LANES)).astype(np.float32)
    return (
        np.concatenate([forward_high, forward_low], axis=1),
        np.concatenate([inverse_high, inverse_high, inverse_low], axis=1),
        np.ascontiguousarray(twist),
    )


def convolve_kernel(
    groups, send_ref, weight_ref, skip_ref, forward_ref, inverse_ref, twist_ref,
    gated_ref, other_ref,
    series, taps, gates, spec_u, spec_h,
    send_sem, recv_sem, pair_sem,
):
    me = lax.axis_index("ctx")
    partner = me + 1 - 2 * lax.rem(me, 2)
    part = send_ref.shape[2]
    blocks = groups * part
    landing = (series, taps, gates)

    barrier = pltpu.get_barrier_semaphore()
    for step in range(1, groups):
        peer = lax.rem(me + step, groups)
        pl.semaphore_signal(barrier, inc=1, device_id={"ctx": peer}, device_id_type=MESH)
    pl.semaphore_wait(barrier, groups - 1)

    def copy_to(which, step):
        peer = lax.rem(me + step, groups)
        return pltpu.make_async_remote_copy(
            src_ref=send_ref.at[which, peer],
            dst_ref=landing[which].at[me],
            send_sem=send_sem.at[which, step],
            recv_sem=recv_sem.at[which, me],
            device_id={"ctx": peer},
            device_id_type=MESH,
        )

    def wait_from(which, step):
        source = lax.rem(me + step, groups)
        pltpu.make_async_remote_copy(
            src_ref=send_ref.at[which, source],
            dst_ref=landing[which].at[source],
            send_sem=send_sem.at[which, step],
            recv_sem=recv_sem.at[which, source],
            device_id={"ctx": source},
            device_id_type=MESH,
        ).wait_recv()

    for which in (0, 1):
        for step in range(1, groups):
            copy_to(which, step).start()
    pair = pltpu.make_async_remote_copy(
        src_ref=weight_ref,
        dst_ref=other_ref,
        send_sem=pair_sem.at[0],
        recv_sem=pair_sem.at[1],
        device_id={"ctx": partner},
        device_id_type=MESH,
    )
    pair.start()
    for step in range(1, groups):
        copy_to(2, step).start()
    for which in range(3):
        landing[which][me] = send_ref[which, me]

    def transform(which, spectrum):
        for step in range(1, groups):
            wait_from(which, step)

        @pl.loop(0, INNER // 2)
        def _(tile):
            columns = pl.ds(pl.multiple_of(tile * 2 * LANES, 2 * LANES), 2 * LANES)
            rows = landing[which][:, :, columns].reshape(blocks, 2 * LANES)
            spectrum[:, columns] = jnp.dot(
                forward_ref[...],
                jnp.concatenate([rows, rows], axis=0),
                preferred_element_type=f32,
            )

    transform(0, spec_u)
    transform(1, spec_h)

    @pl.loop(0, blocks // 8)
    def _(tile):
        real = pl.ds(pl.multiple_of(tile * 8, 8), 8)
        imag = pl.ds(pl.multiple_of(blocks + tile * 8, 8), 8)
        lanes = [slice(b * LANES, (b + 1) * LANES) for b in range(INNER)]
        ur = [spec_u[real, lane] for lane in lanes]
        ui = [spec_u[imag, lane] for lane in lanes]
        hr = [spec_h[real, lane] for lane in lanes]
        hi = [spec_h[imag, lane] for lane in lanes]
        cos, sin = twist_ref[0, real], twist_ref[1, real]

        def term(degree):
            pairs = [(b, degree - b) for b in range(INNER) if 0 <= degree - b < INNER]
            re = sum(ur[b] * hr[d] - ui[b] * hi[d] for b, d in pairs)
            im = sum(ur[b] * hi[d] + ui[b] * hr[d] for b, d in pairs)
            return re, im

        for b in range(INNER):
            re, im = term(b)
            if b + INNER <= 2 * INNER - 2:
                up_re, up_im = term(b + INNER)
                re = re + up_re * cos - up_im * sin
                im = im + up_re * sin + up_im * cos
            spec_u[real, lanes[b]] = re
            spec_u[imag, lanes[b]] = im

    for step in range(1, groups):
        wait_from(2, step)

    @pl.loop(0, INNER // 2)
    def _(tile):
        columns = pl.ds(pl.multiple_of(tile * 2 * LANES, 2 * LANES), 2 * LANES)
        spectrum = spec_u[:, columns]
        high = spectrum.astype(bf16)
        low = (spectrum - high.astype(f32)).astype(bf16)
        convolved = jnp.dot(
            inverse_ref[...],
            jnp.concatenate([high, low, high], axis=0),
            preferred_element_type=f32,
        )
        mixed = series[:, :, columns].reshape(blocks, 2 * LANES).astype(f32)
        gate = gates[:, :, columns].reshape(blocks, 2 * LANES).astype(f32)
        gated_ref[:, columns] = (gate * (convolved + skip_ref[:, columns] * mixed)).astype(bf16)

    for which in range(3):
        for step in range(1, groups):
            copy_to(which, step).wait_send()
    pair.wait()


def project_kernel(
    groups, gated_ref, own_ref, other_ref, out_ref,
    landed, operand, total, sending, chip_in, far_out, far_in, final,
    send_sem, recv_sem, chip_send, chip_recv, far_sem, last_sem, local_sem,
):
    me, mine = lax.axis_index("ctx"), lax.axis_index("tp")
    plane, side = me // 2, lax.rem(me, 2)
    chip, core = mine // 2, lax.rem(mine, 2)
    part = landed.shape[2]
    half = own_ref.shape[1]
    tokens = part * INNER
    sibling = chip * 2 + 1 - core
    across = (1 - chip) * 2 + core
    order = (
        2 * (1 - core) + 1 - chip,
        2 * (1 - core) + chip,
        2 * core + 1 - chip,
        2 * core + chip,
    )
    last_block = order[3]
    to_ctx, to_tp = last_block * 2 + side, plane
    from_ctx, from_tp = mine * 2 + side, 2 * lax.rem(plane, 2) + plane // 2
    stays = jnp.logical_and(to_ctx == me, to_tp == mine)
    leaves = jnp.logical_not(stays)

    barrier = pltpu.get_barrier_semaphore()
    for step in range(1, groups):
        peer = lax.rem(me + step, groups)
        pl.semaphore_signal(barrier, inc=1, device_id={"ctx": peer}, device_id_type=MESH)
    for peer in (sibling, across):
        pl.semaphore_signal(barrier, inc=1, device_id={"tp": peer}, device_id_type=MESH)

    @pl.when(leaves)
    def _():
        pl.semaphore_signal(
            barrier, inc=1, device_id={"ctx": from_ctx, "tp": from_tp}, device_id_type=MESH
        )

    pl.semaphore_wait(barrier, groups + 1 + leaves.astype(jnp.int32))

    def rows_of(index, towards):
        return pl.ds(pl.multiple_of((order[index] * 2 + lax.rem(towards, 2)) * part, part), part)

    def copy_to(index, step):
        peer = lax.rem(me + step, groups)
        return pltpu.make_async_remote_copy(
            src_ref=gated_ref.at[rows_of(index, peer)],
            dst_ref=landed.at[index, me],
            send_sem=send_sem.at[index, step],
            recv_sem=recv_sem.at[index, me],
            device_id={"ctx": peer},
            device_id_type=MESH,
        )

    for index in range(4):
        for step in range(1, groups):
            copy_to(index, step).start()
    for index in range(4):
        landed[index, me] = gated_ref[rows_of(index, me)]

    def partial(index):
        for step in range(1, groups):
            source = lax.rem(me + step, groups)
            pltpu.make_async_remote_copy(
                src_ref=landed.at[index, source],
                dst_ref=landed.at[index, source],
                send_sem=send_sem.at[index, step],
                recv_sem=recv_sem.at[index, source],
                device_id={"ctx": source},
                device_id_type=MESH,
            ).wait_recv()
        for source in range(groups):
            for b in range(INNER):
                operand[b * part : (b + 1) * part, source * LANES : (source + 1) * LANES] = landed[
                    index, source, :, b * LANES : (b + 1) * LANES
                ]
        for weight, which in ((own_ref, side), (other_ref, 1 - side)):
            columns = pl.ds(pl.multiple_of(which * half, half), half)
            total[:, columns] = jnp.dot(operand[...], weight[...], preferred_element_type=f32)

    def to_sibling(index):
        return pltpu.make_async_remote_copy(
            src_ref=sending.at[index],
            dst_ref=chip_in.at[index],
            send_sem=chip_send.at[index],
            recv_sem=chip_recv.at[index],
            device_id={"tp": sibling},
            device_id_type=MESH,
        )

    for index in range(2):
        partial(index)
        sending[index] = total[...].astype(bf16)
        to_sibling(index).start()

    partial(2)
    to_sibling(0).wait_recv()
    far_out[...] = (total[...] + chip_in[0].astype(f32)).astype(bf16)
    far = pltpu.make_async_remote_copy(
        src_ref=far_out,
        dst_ref=far_in,
        send_sem=far_sem.at[0],
        recv_sem=far_sem.at[1],
        device_id={"tp": across},
        device_id_type=MESH,
    )
    far.start()

    partial(3)
    to_sibling(1).wait_recv()
    far.wait_recv()
    final[...] = (total[...] + chip_in[1].astype(f32) + far_in[...].astype(f32)).astype(bf16)

    @pl.when(leaves)
    def _():
        last = pltpu.make_async_remote_copy(
            src_ref=final,
            dst_ref=out_ref,
            send_sem=last_sem.at[0],
            recv_sem=last_sem.at[1],
            device_id={"ctx": to_ctx, "tp": to_tp},
            device_id_type=MESH,
        )
        last.start()
        last.wait()

    @pl.when(stays)
    def _():
        keep = pltpu.make_async_copy(final, out_ref, local_sem)
        keep.start()
        keep.wait()

    for index in range(4):
        for step in range(1, groups):
            copy_to(index, step).wait_send()
    for index in range(2):
        to_sibling(index).wait_send()
    far.wait_send()


def kernel_path(query_rows, key_rows, value_rows, filters, skip_gain, out_weight):
    row_count, chan_count = key_rows.shape
    groups = lax.axis_size("ctx")
    me = lax.axis_index("ctx")
    part = row_count // INNER
    wide = INNER * LANES
    blocks = groups * part
    half = out_weight.shape[1]
    mixed_in = (key_rows.astype(f32) * value_rows.astype(f32)).astype(bf16)

    def by_group(rows):
        cut = rows.reshape(part, INNER, groups, LANES)
        return cut.transpose(2, 0, 1, 3).reshape(groups, part, wide)

    sent = jnp.stack([by_group(mixed_in), by_group(filters), by_group(query_rows)])
    skip = jnp.tile(lax.dynamic_slice(skip_gain, (me * LANES,), (LANES,)), INNER)[None, :]
    forward, inverse, twist = block_tables(blocks)
    vmem = pl.BlockSpec(memory_space=pltpu.VMEM)
    hbm = pl.BlockSpec(memory_space=pl.ANY)
    dma = pltpu.SemaphoreType.DMA
    gated, other = pl.pallas_call(
        functools.partial(convolve_kernel, groups),
        out_shape=(
            jax.ShapeDtypeStruct((blocks, wide), bf16),
            jax.ShapeDtypeStruct(out_weight.shape, bf16),
        ),
        in_specs=[vmem, hbm, vmem, vmem, vmem, vmem],
        out_specs=(vmem, hbm),
        scratch_shapes=[
            pltpu.VMEM((groups, part, wide), bf16),
            pltpu.VMEM((groups, part, wide), bf16),
            pltpu.VMEM((groups, part, wide), bf16),
            pltpu.VMEM((2 * blocks, wide), f32),
            pltpu.VMEM((2 * blocks, wide), f32),
            dma((3, groups)),
            dma((3, groups)),
            dma((2,)),
        ],
        compiler_params=pltpu.CompilerParams(
            collective_id=0, has_side_effects=True, vmem_limit_bytes=40 * 2**20
        ),
        name="convolve",
    )(sent, out_weight, skip, jnp.asarray(forward), jnp.asarray(inverse), jnp.asarray(twist))
    result = pl.pallas_call(
        functools.partial(project_kernel, groups),
        out_shape=jax.ShapeDtypeStruct((row_count, 2 * half), bf16),
        in_specs=[vmem, vmem, vmem],
        out_specs=hbm,
        scratch_shapes=[
            pltpu.VMEM((4, groups, part, wide), bf16),
            pltpu.VMEM((row_count, chan_count), bf16),
            pltpu.VMEM((row_count, 2 * half), f32),
            pltpu.VMEM((2, row_count, 2 * half), bf16),
            pltpu.VMEM((2, row_count, 2 * half), bf16),
            pltpu.VMEM((row_count, 2 * half), bf16),
            pltpu.VMEM((row_count, 2 * half), bf16),
            pltpu.VMEM((row_count, 2 * half), bf16),
            dma((4, groups)),
            dma((4, groups)),
            dma((2,)),
            dma((2,)),
            dma((2,)),
            dma((2,)),
            dma,
        ],
        compiler_params=pltpu.CompilerParams(
            collective_id=1, has_side_effects=True, vmem_limit_bytes=40 * 2**20
        ),
        name="project",
    )(gated, out_weight, other)
    return result.reshape(INNER, part, 2 * half).transpose(1, 0, 2).reshape(row_count, 2 * half)


def on_device(query_rows, key_rows, value_rows, filters, skip_gain, out_weight):
    row_count, chan_count = key_rows.shape
    groups, shares = lax.axis_size("ctx"), lax.axis_size("tp")
    fits = (
        shares == 4
        and groups == 2 * shares
        and chan_count == groups * LANES
        and row_count % (16 * INNER) == 0
        and groups * row_count <= 2048
    )
    path = kernel_path if fits else plain_path
    return path(query_rows, key_rows, value_rows, filters, skip_gain, out_weight)


def solution(mesh):
    in_specs = (
        P("ctx", "tp"),
        P("ctx", "tp"),
        P("ctx", "tp"),
        P("ctx", "tp"),
        P("tp"),
        P("tp", "ctx"),
    )
    out_specs = P("ctx", "tp")
    return jax.shard_map(
        on_device, mesh=mesh, in_specs=in_specs, out_specs=out_specs, check_vma=False
    )
```

```python
import functools
import math

import jax
import jax.numpy as jnp
import ml_dtypes
import numpy as np
from jax import lax
from jax.experimental import pallas as pl
from jax.experimental.pallas import tpu as pltpu
from jax.sharding import PartitionSpec as P

precise = lax.Precision.HIGHEST
MESH = pl.DeviceIdType.MESH
LANES = 128
INNER = 8
f32 = jnp.float32
bf16 = jnp.bfloat16


def make_tables(full_len, size_one, second):
    index_one = jnp.arange(size_one, dtype=jnp.int32)
    half_one = jnp.arange(size_one // 2, dtype=jnp.int32)
    index_two = jnp.arange(second, dtype=jnp.int32)
    angle_one = (
        2.0
        * math.pi
        / size_one
        * (index_one[:, None] * half_one[None, :] % size_one).astype(jnp.float32)
    )
    angle_two = (
        2.0
        * math.pi
        / second
        * (index_two[:, None] * index_two[None, :] % second).astype(jnp.float32)
    )
    angle_mid = (
        2.0
        * math.pi
        / full_len
        * (index_one[:, None] * index_two[None, :] % full_len).astype(jnp.float32)
    )
    return (
        jnp.cos(angle_one),
        jnp.sin(angle_one),
        jnp.cos(angle_two),
        jnp.sin(angle_two),
        jnp.cos(angle_mid),
        jnp.sin(angle_mid),
    )


def along_second(matrix, table):
    return jnp.einsum("mkb,bj->mkj", matrix, table, precision=precise)


def forward_spectrum(signal, tables, size_one, second):
    cos_one, sin_one, cos_two, sin_two, cos_mid, sin_mid = tables
    reshaped = signal.reshape(signal.shape[0], size_one // 2, second)
    real_a = jnp.einsum("ka,mab->mkb", cos_one, reshaped, precision=precise)
    imag_a = -jnp.einsum("ka,mab->mkb", sin_one, reshaped, precision=precise)
    real_b = real_a * cos_mid + imag_a * sin_mid
    imag_b = imag_a * cos_mid - real_a * sin_mid
    real_c = along_second(real_b, cos_two) + along_second(imag_b, sin_two)
    imag_c = along_second(imag_b, cos_two) - along_second(real_b, sin_two)
    return (real_c, imag_c)


def inverse_signal(real_p, imag_p, tables, full_len):
    cos_one, sin_one, cos_two, sin_two, cos_mid, sin_mid = tables
    real_q = along_second(real_p, cos_two) - along_second(imag_p, sin_two)
    imag_q = along_second(imag_p, cos_two) + along_second(real_p, sin_two)
    real_r = real_q * cos_mid - imag_q * sin_mid
    imag_r = real_q * sin_mid + imag_q * cos_mid
    result = jnp.einsum("ka,mkb->mab", cos_one, real_r, precision=precise) - jnp.einsum(
        "ka,mkb->mab", sin_one, imag_r, precision=precise
    )
    return (result / full_len).reshape(real_p.shape[0], full_len // 2)


def convolve_block(series, taps):
    length = series.shape[-1]
    full_len = 2 * length
    size_one = 1 << (full_len.bit_length() - 1) // 2
    second = full_len // size_one
    tables = make_tables(full_len, size_one, second)
    channels = series.shape[0]
    stacked = jnp.concatenate([series.astype(jnp.float32), taps.astype(jnp.float32)], axis=0)
    real_s, imag_s = forward_spectrum(stacked, tables, size_one, second)
    real_u, real_h = (real_s[:channels], real_s[channels:])
    imag_u, imag_h = (imag_s[:channels], imag_s[channels:])
    real_p = real_u * real_h - imag_u * imag_h
    imag_p = real_u * imag_h + imag_u * real_h
    return inverse_signal(real_p, imag_p, tables, full_len)


def plain_path(query_rows, key_rows, value_rows, filters, skip_gain, out_weight):
    row_count, chan_count = key_rows.shape
    groups = lax.axis_size("ctx")
    per_group = chan_count // groups
    mixed_in = (key_rows.astype(jnp.float32) * value_rows.astype(jnp.float32)).astype(jnp.bfloat16)
    series_t = mixed_in.T.reshape(groups, per_group, row_count)
    taps_t = filters.T.reshape(groups, per_group, row_count)
    series_p = lax.all_to_all(series_t, "ctx", split_axis=0, concat_axis=2, tiled=True)
    taps_p = lax.all_to_all(taps_t, "ctx", split_axis=0, concat_axis=2, tiled=True)
    result = convolve_block(series_p[0], taps_p[0])[None]
    returned = lax.all_to_all(result, "ctx", split_axis=2, concat_axis=0, tiled=True)
    convolved = returned.reshape(chan_count, row_count).T
    gated_rows = (
        query_rows.astype(jnp.float32)
        * (convolved + skip_gain[None, :] * mixed_in.astype(jnp.float32))
    ).astype(jnp.bfloat16)
    partial_value = jnp.dot(
        gated_rows,
        lax.all_gather(out_weight, "ctx", axis=1, tiled=True),
        preferred_element_type=jnp.float32,
    )
    return lax.psum_scatter(partial_value, "tp", scatter_dimension=1, tiled=True).astype(
        jnp.bfloat16
    )


def split_table(table):
    high = table.astype(ml_dtypes.bfloat16)
    low = (table - high.astype(np.float64)).astype(ml_dtypes.bfloat16)
    return high, low


def block_tables(blocks):
    angle = np.pi * (np.arange(blocks) + 0.5) / blocks
    phase = np.outer(angle, np.arange(blocks))
    forward = np.concatenate([np.cos(phase), -np.sin(phase)], axis=0)
    inverse = np.concatenate([np.cos(phase.T), -np.sin(phase.T)], axis=1) / blocks
    forward_high, forward_low = split_table(forward)
    inverse_high, inverse_low = split_table(inverse)
    twist = np.stack([np.cos(angle), -np.sin(angle)])[:, :, None]
    twist = np.broadcast_to(twist, (2, blocks, LANES)).astype(np.float32)
    return (
        np.concatenate([forward_high, forward_low], axis=1),
        np.concatenate([inverse_high, inverse_high, inverse_low], axis=1),
        np.ascontiguousarray(twist),
    )


def mixer_kernel(
    groups, send_ref, own_ref, skip_ref, forward_ref, inverse_ref, twist_ref, out_ref,
    series, taps, gates, spec_u, spec_h, gated_ref, other_ref,
    landed, operand, total, sending, chip_in, far_out, far_in, final,
    send_sem, recv_sem, pair_send, pair_recv, piece_send, piece_recv, pass_send,
    chip_send, chip_recv, far_send, far_recv, last_send, last_recv, local_sem,
):
    me, mine = lax.axis_index("ctx"), lax.axis_index("tp")
    plane, side = me // 2, lax.rem(me, 2)
    chip, core = mine // 2, lax.rem(mine, 2)
    partner = plane * 2 + 1 - side
    near = plane + 1 - 2 * lax.rem(plane, 2)
    beyond = lax.rem(plane + 2, groups // 2)
    mate = near * 2 + side
    part = send_ref.shape[2]
    blocks = groups * part
    depth, half = own_ref.shape
    splits, small = landed.shape[0], landed.shape[3]
    landing = (series, taps, gates)
    sibling = chip * 2 + 1 - core
    opposite = (1 - chip) * 2 + core
    order = (
        2 * (1 - core) + 1 - chip,
        2 * (1 - core) + chip,
        2 * core + 1 - chip,
        2 * core + chip,
    )
    to_ctx, to_tp = order[3] * 2 + side, plane
    from_ctx, from_tp = mine * 2 + side, 2 * lax.rem(plane, 2) + plane // 2
    stays = jnp.logical_and(to_ctx == me, to_tp == mine)
    leaves = jnp.logical_not(stays)

    barrier = pltpu.get_barrier_semaphore()
    for step in range(1, groups):
        peer = lax.rem(me + step, groups)
        pl.semaphore_signal(barrier, inc=1, device_id={"ctx": peer}, device_id_type=MESH)
    for peer in (sibling, opposite):
        pl.semaphore_signal(barrier, inc=1, device_id={"tp": peer}, device_id_type=MESH)

    @pl.when(leaves)
    def _():
        pl.semaphore_signal(
            barrier, inc=1, device_id={"ctx": from_ctx, "tp": from_tp}, device_id_type=MESH
        )

    pl.semaphore_wait(barrier, groups + 1 + leaves.astype(jnp.int32))

    def copy_to(which, step):
        peer = lax.rem(me + step, groups)
        return pltpu.make_async_remote_copy(
            src_ref=send_ref.at[which, peer],
            dst_ref=landing[which].at[me],
            send_sem=send_sem.at[which, step],
            recv_sem=recv_sem.at[which, me],
            device_id={"ctx": peer},
            device_id_type=MESH,
        )

    def wait_from(which, step):
        source = lax.rem(me + step, groups)
        pltpu.make_async_remote_copy(
            src_ref=send_ref.at[which, source],
            dst_ref=landing[which].at[source],
            send_sem=send_sem.at[which, step],
            recv_sem=recv_sem.at[which, source],
            device_id={"ctx": source},
            device_id_type=MESH,
        ).wait_recv()

    def weight_copy(which):
        rows = pl.ds(which * (depth // 2), depth // 2)
        return pltpu.make_async_remote_copy(
            src_ref=own_ref.at[rows],
            dst_ref=other_ref.at[rows],
            send_sem=pair_send.at[which],
            recv_sem=pair_recv.at[which],
            device_id={"ctx": partner},
            device_id_type=MESH,
        )

    for which in (0, 1):
        for step in range(1, groups):
            copy_to(which, step).start()
    weight_copy(0).start()
    for which in range(3):
        landing[which][me] = send_ref[which, me]

    def transform(which, spectrum):
        @pl.loop(0, INNER // 2)
        def _(tile):
            columns = pl.ds(pl.multiple_of(tile * 2 * LANES, 2 * LANES), 2 * LANES)
            rows = landing[which][:, :, columns].reshape(blocks, 2 * LANES)
            spectrum[:, columns] = jnp.dot(
                forward_ref[...],
                jnp.concatenate([rows, rows], axis=0),
                preferred_element_type=f32,
            )

    for step in range(1, groups):
        wait_from(0, step)
    transform(0, spec_u)
    for step in range(1, groups):
        wait_from(1, step)
        if step == groups // 2:
            for later in range(1, groups):
                copy_to(2, later).start()
    weight_copy(1).start()
    transform(1, spec_h)

    @pl.loop(0, blocks // 8)
    def _(tile):
        real = pl.ds(pl.multiple_of(tile * 8, 8), 8)
        imag = pl.ds(pl.multiple_of(blocks + tile * 8, 8), 8)
        lanes = [slice(b * LANES, (b + 1) * LANES) for b in range(INNER)]
        ur = [spec_u[real, lane] for lane in lanes]
        ui = [spec_u[imag, lane] for lane in lanes]
        hr = [spec_h[real, lane] for lane in lanes]
        hi = [spec_h[imag, lane] for lane in lanes]
        cos, sin = twist_ref[0, real], twist_ref[1, real]

        def term(degree):
            pairs = [(b, degree - b) for b in range(INNER) if 0 <= degree - b < INNER]
            re = sum(ur[b] * hr[d] - ui[b] * hi[d] for b, d in pairs)
            im = sum(ur[b] * hi[d] + ui[b] * hr[d] for b, d in pairs)
            return re, im

        for b in range(INNER):
            re, im = term(b)
            if b + INNER <= 2 * INNER - 2:
                up_re, up_im = term(b + INNER)
                re = re + up_re * cos - up_im * sin
                im = im + up_re * sin + up_im * cos
            spec_u[real, lanes[b]] = re
            spec_u[imag, lanes[b]] = im

    for step in range(1, groups):
        wait_from(2, step)

    @pl.loop(0, INNER // 2)
    def _(tile):
        columns = pl.ds(pl.multiple_of(tile * 2 * LANES, 2 * LANES), 2 * LANES)
        spectrum = spec_u[:, columns]
        high = spectrum.astype(bf16)
        low = (spectrum - high.astype(f32)).astype(bf16)
        convolved = jnp.dot(
            inverse_ref[...],
            jnp.concatenate([high, low, high], axis=0),
            preferred_element_type=f32,
        )
        mixed = series[:, :, columns].reshape(blocks, 2 * LANES).astype(f32)
        gate = gates[:, :, columns].reshape(blocks, 2 * LANES).astype(f32)
        gated_ref[:, columns] = (gate * (convolved + skip_ref[:, columns] * mixed)).astype(bf16)

    pieces = [(split, index) for split in range(splits) for index in range(4)]
    direct = (
        beyond * 2 + side, beyond * 2 + 1 - side,
        near * 2 + side, near * 2 + 1 - side,
        partner,
    )

    def rows_of(piece, towards):
        split, index = piece
        start = (order[index] * 2 + lax.rem(towards, 2)) * part + split * small
        return pl.ds(pl.multiple_of(start, small), small)

    def piece_to(piece, slot):
        return pltpu.make_async_remote_copy(
            src_ref=gated_ref.at[rows_of(piece, direct[slot])],
            dst_ref=landed.at[piece[0], piece[1], me],
            send_sem=piece_send.at[piece[0], piece[1], slot],
            recv_sem=piece_recv.at[piece[0], piece[1], me],
            device_id={"ctx": direct[slot]},
            device_id_type=MESH,
        )

    def pass_on(piece, source, slot):
        place = landed.at[piece[0], piece[1], source]
        return pltpu.make_async_remote_copy(
            src_ref=place,
            dst_ref=place,
            send_sem=pass_send.at[piece[0], piece[1], slot],
            recv_sem=piece_recv.at[piece[0], piece[1], source],
            device_id={"ctx": mate},
            device_id_type=MESH,
        )

    def launch(piece):
        for slot in range(5):
            piece_to(piece, slot).start()
        landed[piece[0], piece[1], me] = gated_ref[rows_of(piece, me)]

    def forward(piece):
        for slot in range(2):
            copy = pass_on(piece, direct[slot], slot)
            copy.wait_recv()
            copy.start()

    far_plane = lax.rem(near + 2, groups // 2)
    passed = (far_plane * 2 + side, far_plane * 2 + 1 - side)

    def partial(piece):
        for source in direct[2:] + passed:
            pass_on(piece, source, 0).wait_recv()
        for source in range(groups):
            for b in range(INNER):
                operand[b * small : (b + 1) * small, source * LANES : (source + 1) * LANES] = landed[
                    piece[0], piece[1], source, :, b * LANES : (b + 1) * LANES
                ]
        for weight, which in ((own_ref, side), (other_ref, 1 - side)):
            columns = pl.ds(pl.multiple_of(which * half, half), half)
            total[:, columns] = jnp.dot(operand[...], weight[...], preferred_element_type=f32)

    def to_sibling(split, index):
        return pltpu.make_async_remote_copy(
            src_ref=sending.at[split, index],
            dst_ref=chip_in.at[split, index],
            send_sem=chip_send.at[split, index],
            recv_sem=chip_recv.at[split, index],
            device_id={"tp": sibling},
            device_id_type=MESH,
        )

    def to_opposite(split):
        return pltpu.make_async_remote_copy(
            src_ref=far_out.at[split],
            dst_ref=far_in.at[split],
            send_sem=far_send.at[split],
            recv_sem=far_recv.at[split],
            device_id={"tp": opposite},
            device_id_type=MESH,
        )

    def to_owner(split):
        return pltpu.make_async_remote_copy(
            src_ref=final.at[split],
            dst_ref=out_ref.at[split],
            send_sem=last_send.at[split],
            recv_sem=last_recv.at[split],
            device_id={"ctx": to_ctx, "tp": to_tp},
            device_id_type=MESH,
        )

    def keep(split):
        return pltpu.make_async_copy(final.at[split], out_ref.at[split], local_sem.at[split])

    window = 3
    for piece in pieces[:window]:
        launch(piece)
    forward(pieces[0])
    weight_copy(0).wait_recv()
    weight_copy(1).wait_recv()
    for number, piece in enumerate(pieces):
        split, index = piece
        if number + window < len(pieces):
            launch(pieces[number + window])
        if number + 1 < len(pieces):
            forward(pieces[number + 1])
        partial(piece)
        if index < 2:
            sending[split, index] = total[...].astype(bf16)
            to_sibling(split, index).start()
        elif index == 2:
            to_sibling(split, 0).wait_recv()
            far_out[split] = (total[...] + chip_in[split, 0].astype(f32)).astype(bf16)
            to_opposite(split).start()
        else:
            to_sibling(split, 1).wait_recv()
            to_opposite(split).wait_recv()
            final[split] = (
                total[...] + chip_in[split, 1].astype(f32) + far_in[split].astype(f32)
            ).astype(bf16)

            @pl.when(leaves)
            def _():
                to_owner(split).start()

            @pl.when(stays)
            def _():
                keep(split).start()

    for which in range(3):
        for step in range(1, groups):
            copy_to(which, step).wait_send()
    for piece in pieces:
        for slot in range(5):
            piece_to(piece, slot).wait_send()
        for slot in range(2):
            pass_on(piece, direct[slot], slot).wait_send()
    for which in range(2):
        weight_copy(which).wait_send()
    for split in range(splits):
        for index in range(2):
            to_sibling(split, index).wait_send()
        to_opposite(split).wait_send()

        @pl.when(leaves)
        def _():
            to_owner(split).wait()

        @pl.when(stays)
        def _():
            keep(split).wait()


def kernel_path(query_rows, key_rows, value_rows, filters, skip_gain, out_weight):
    row_count, chan_count = key_rows.shape
    groups = lax.axis_size("ctx")
    me = lax.axis_index("ctx")
    part = row_count // INNER
    small = 16
    splits = part // small
    piece = small * INNER
    wide = INNER * LANES
    blocks = groups * part
    depth, half = out_weight.shape
    mixed_in = (key_rows.astype(f32) * value_rows.astype(f32)).astype(bf16)

    def by_group(rows):
        cut = rows.reshape(part, INNER, groups, LANES)
        return cut.transpose(2, 0, 1, 3).reshape(groups, part, wide)

    sent = jnp.stack([by_group(mixed_in), by_group(filters), by_group(query_rows)])
    skip = jnp.tile(lax.dynamic_slice(skip_gain, (me * LANES,), (LANES,)), INNER)[None, :]
    forward, inverse, twist = block_tables(blocks)
    vmem = pl.BlockSpec(memory_space=pltpu.VMEM)
    dma = pltpu.SemaphoreType.DMA
    result = pl.pallas_call(
        functools.partial(mixer_kernel, groups),
        out_shape=jax.ShapeDtypeStruct((splits, piece, 2 * half), bf16),
        in_specs=[vmem] * 6,
        out_specs=pl.BlockSpec(memory_space=pl.ANY),
        scratch_shapes=[
            pltpu.VMEM((groups, part, wide), bf16),
            pltpu.VMEM((groups, part, wide), bf16),
            pltpu.VMEM((groups, part, wide), bf16),
            pltpu.VMEM((2 * blocks, wide), f32),
            pltpu.VMEM((2 * blocks, wide), f32),
            pltpu.VMEM((blocks, wide), bf16),
            pltpu.VMEM((depth, half), bf16),
            pltpu.VMEM((splits, 4, groups, small, wide), bf16),
            pltpu.VMEM((piece, chan_count), bf16),
            pltpu.VMEM((piece, 2 * half), f32),
            pltpu.VMEM((splits, 2, piece, 2 * half), bf16),
            pltpu.VMEM((splits, 2, piece, 2 * half), bf16),
            pltpu.VMEM((splits, piece, 2 * half), bf16),
            pltpu.VMEM((splits, piece, 2 * half), bf16),
            pltpu.VMEM((splits, piece, 2 * half), bf16),
            dma((3, groups)),
            dma((3, groups)),
            dma((2,)),
            dma((2,)),
            dma((splits, 4, 5)),
            dma((splits, 4, groups)),
            dma((splits, 4, 2)),
            dma((splits, 2)),
            dma((splits, 2)),
            dma((splits,)),
            dma((splits,)),
            dma((splits,)),
            dma((splits,)),
            dma((splits,)),
        ],
        compiler_params=pltpu.CompilerParams(
            collective_id=0, has_side_effects=True, vmem_limit_bytes=40 * 2**20
        ),
        name="mixer",
    )(sent, out_weight, skip, jnp.asarray(forward), jnp.asarray(inverse), jnp.asarray(twist))
    result = result.reshape(splits, INNER, small, 2 * half)
    return result.transpose(0, 2, 1, 3).reshape(row_count, 2 * half)


def on_device(query_rows, key_rows, value_rows, filters, skip_gain, out_weight):
    row_count, chan_count = key_rows.shape
    groups, shares = lax.axis_size("ctx"), lax.axis_size("tp")
    fits = (
        shares == 4
        and groups == 2 * shares
        and chan_count == groups * LANES
        and row_count % (16 * INNER) == 0
        and groups * row_count <= 2048
    )
    path = kernel_path if fits else plain_path
    return path(query_rows, key_rows, value_rows, filters, skip_gain, out_weight)


def solution(mesh):
    in_specs = (
        P("ctx", "tp"),
        P("ctx", "tp"),
        P("ctx", "tp"),
        P("ctx", "tp"),
        P("tp"),
        P("tp", "ctx"),
    )
    out_specs = P("ctx", "tp")
    return jax.shard_map(
        on_device, mesh=mesh, in_specs=in_specs, out_specs=out_specs, check_vma=False
    )
```

```python
import functools
import math

import jax
import jax.numpy as jnp
import ml_dtypes
import numpy as np
from jax import lax
from jax.experimental import pallas as pl
from jax.experimental.pallas import tpu as pltpu
from jax.sharding import PartitionSpec as P

precise = lax.Precision.HIGHEST
MESH = pl.DeviceIdType.MESH
LANES = 128
INNER = 8
f32 = jnp.float32
bf16 = jnp.bfloat16


def make_tables(full_len, size_one, second):
    index_one = jnp.arange(size_one, dtype=jnp.int32)
    half_one = jnp.arange(size_one // 2, dtype=jnp.int32)
    index_two = jnp.arange(second, dtype=jnp.int32)
    angle_one = (
        2.0
        * math.pi
        / size_one
        * (index_one[:, None] * half_one[None, :] % size_one).astype(jnp.float32)
    )
    angle_two = (
        2.0
        * math.pi
        / second
        * (index_two[:, None] * index_two[None, :] % second).astype(jnp.float32)
    )
    angle_mid = (
        2.0
        * math.pi
        / full_len
        * (index_one[:, None] * index_two[None, :] % full_len).astype(jnp.float32)
    )
    return (
        jnp.cos(angle_one),
        jnp.sin(angle_one),
        jnp.cos(angle_two),
        jnp.sin(angle_two),
        jnp.cos(angle_mid),
        jnp.sin(angle_mid),
    )


def along_second(matrix, table):
    return jnp.einsum("mkb,bj->mkj", matrix, table, precision=precise)


def forward_spectrum(signal, tables, size_one, second):
    cos_one, sin_one, cos_two, sin_two, cos_mid, sin_mid = tables
    reshaped = signal.reshape(signal.shape[0], size_one // 2, second)
    real_a = jnp.einsum("ka,mab->mkb", cos_one, reshaped, precision=precise)
    imag_a = -jnp.einsum("ka,mab->mkb", sin_one, reshaped, precision=precise)
    real_b = real_a * cos_mid + imag_a * sin_mid
    imag_b = imag_a * cos_mid - real_a * sin_mid
    real_c = along_second(real_b, cos_two) + along_second(imag_b, sin_two)
    imag_c = along_second(imag_b, cos_two) - along_second(real_b, sin_two)
    return (real_c, imag_c)


def inverse_signal(real_p, imag_p, tables, full_len):
    cos_one, sin_one, cos_two, sin_two, cos_mid, sin_mid = tables
    real_q = along_second(real_p, cos_two) - along_second(imag_p, sin_two)
    imag_q = along_second(imag_p, cos_two) + along_second(real_p, sin_two)
    real_r = real_q * cos_mid - imag_q * sin_mid
    imag_r = real_q * sin_mid + imag_q * cos_mid
    result = jnp.einsum("ka,mkb->mab", cos_one, real_r, precision=precise) - jnp.einsum(
        "ka,mkb->mab", sin_one, imag_r, precision=precise
    )
    return (result / full_len).reshape(real_p.shape[0], full_len // 2)


def convolve_block(series, taps):
    length = series.shape[-1]
    full_len = 2 * length
    size_one = 1 << (full_len.bit_length() - 1) // 2
    second = full_len // size_one
    tables = make_tables(full_len, size_one, second)
    channels = series.shape[0]
    stacked = jnp.concatenate([series.astype(jnp.float32), taps.astype(jnp.float32)], axis=0)
    real_s, imag_s = forward_spectrum(stacked, tables, size_one, second)
    real_u, real_h = (real_s[:channels], real_s[channels:])
    imag_u, imag_h = (imag_s[:channels], imag_s[channels:])
    real_p = real_u * real_h - imag_u * imag_h
    imag_p = real_u * imag_h + imag_u * real_h
    return inverse_signal(real_p, imag_p, tables, full_len)


def plain_path(query_rows, key_rows, value_rows, filters, skip_gain, out_weight):
    row_count, chan_count = key_rows.shape
    groups = lax.axis_size("ctx")
    per_group = chan_count // groups
    mixed_in = (key_rows.astype(jnp.float32) * value_rows.astype(jnp.float32)).astype(jnp.bfloat16)
    series_t = mixed_in.T.reshape(groups, per_group, row_count)
    taps_t = filters.T.reshape(groups, per_group, row_count)
    series_p = lax.all_to_all(series_t, "ctx", split_axis=0, concat_axis=2, tiled=True)
    taps_p = lax.all_to_all(taps_t, "ctx", split_axis=0, concat_axis=2, tiled=True)
    result = convolve_block(series_p[0], taps_p[0])[None]
    returned = lax.all_to_all(result, "ctx", split_axis=2, concat_axis=0, tiled=True)
    convolved = returned.reshape(chan_count, row_count).T
    gated_rows = (
        query_rows.astype(jnp.float32)
        * (convolved + skip_gain[None, :] * mixed_in.astype(jnp.float32))
    ).astype(jnp.bfloat16)
    partial_value = jnp.dot(
        gated_rows,
        lax.all_gather(out_weight, "ctx", axis=1, tiled=True),
        preferred_element_type=jnp.float32,
    )
    return lax.psum_scatter(partial_value, "tp", scatter_dimension=1, tiled=True).astype(
        jnp.bfloat16
    )


def split_table(table):
    high = table.astype(ml_dtypes.bfloat16)
    low = (table - high.astype(np.float64)).astype(ml_dtypes.bfloat16)
    return high, low


def block_tables(blocks):
    angle = np.pi * (np.arange(blocks) + 0.5) / blocks
    phase = np.outer(angle, np.arange(blocks))
    forward = np.concatenate([np.cos(phase), -np.sin(phase)], axis=0)
    inverse = np.concatenate([np.cos(phase.T), -np.sin(phase.T)], axis=1) / blocks
    forward_high, forward_low = split_table(forward)
    inverse_high, inverse_low = split_table(inverse)
    twist = np.stack([np.cos(angle), -np.sin(angle)])[:, :, None]
    twist = np.broadcast_to(twist, (2, blocks, LANES)).astype(np.float32)
    return (
        np.concatenate([forward_high, forward_low], axis=1),
        np.concatenate([inverse_high, inverse_high, inverse_low], axis=1),
        np.ascontiguousarray(twist),
    )


def mixer_kernel(
    groups, send_ref, own_ref, skip_ref, forward_ref, inverse_ref, twist_ref, out_ref,
    series, taps, gates, spec_u, spec_h, gated_ref, other_ref,
    landed, operand, total, sending, chip_in, far_out, far_in, final,
    send_sem, recv_sem, pair_send, pair_recv, piece_send, piece_recv, pass_send,
    chip_send, chip_recv, far_send, far_recv, last_send, last_recv, local_sem,
):
    me, mine = lax.axis_index("ctx"), lax.axis_index("tp")
    plane, side = me // 2, lax.rem(me, 2)
    chip, core = mine // 2, lax.rem(mine, 2)
    partner = plane * 2 + 1 - side
    near = plane + 1 - 2 * lax.rem(plane, 2)
    beyond = lax.rem(plane + 2, groups // 2)
    mate = near * 2 + side
    part = send_ref.shape[2]
    blocks = groups * part
    depth, half = own_ref.shape
    splits, small = landed.shape[0], landed.shape[3]
    landing = (series, taps, gates)
    sibling = chip * 2 + 1 - core
    opposite = (1 - chip) * 2 + core
    order = (
        2 * (1 - core) + 1 - chip,
        2 * (1 - core) + chip,
        2 * core + 1 - chip,
        2 * core + chip,
    )
    to_ctx, to_tp = order[3] * 2 + side, plane
    from_ctx, from_tp = mine * 2 + side, 2 * lax.rem(plane, 2) + plane // 2
    stays = jnp.logical_and(to_ctx == me, to_tp == mine)
    leaves = jnp.logical_not(stays)

    barrier = pltpu.get_barrier_semaphore()
    for step in range(1, groups):
        peer = lax.rem(me + step, groups)
        pl.semaphore_signal(barrier, inc=1, device_id={"ctx": peer}, device_id_type=MESH)
    for peer in (sibling, opposite):
        pl.semaphore_signal(barrier, inc=1, device_id={"tp": peer}, device_id_type=MESH)

    @pl.when(leaves)
    def _():
        pl.semaphore_signal(
            barrier, inc=1, device_id={"ctx": from_ctx, "tp": from_tp}, device_id_type=MESH
        )

    pl.semaphore_wait(barrier, groups + 1 + leaves.astype(jnp.int32))

    def copy_to(which, step):
        peer = lax.rem(me + step, groups)
        return pltpu.make_async_remote_copy(
            src_ref=send_ref.at[which, peer],
            dst_ref=landing[which].at[me],
            send_sem=send_sem.at[which, step],
            recv_sem=recv_sem.at[which, me],
            device_id={"ctx": peer},
            device_id_type=MESH,
        )

    def wait_from(which, step):
        source = lax.rem(me + step, groups)
        pltpu.make_async_remote_copy(
            src_ref=send_ref.at[which, source],
            dst_ref=landing[which].at[source],
            send_sem=send_sem.at[which, step],
            recv_sem=recv_sem.at[which, source],
            device_id={"ctx": source},
            device_id_type=MESH,
        ).wait_recv()

    def weight_copy(which):
        rows = pl.ds(which * (depth // 2), depth // 2)
        return pltpu.make_async_remote_copy(
            src_ref=own_ref.at[rows],
            dst_ref=other_ref.at[rows],
            send_sem=pair_send.at[which],
            recv_sem=pair_recv.at[which],
            device_id={"ctx": partner},
            device_id_type=MESH,
        )

    for which in (0, 1):
        for step in range(1, groups):
            copy_to(which, step).start()
    weight_copy(0).start()
    for which in range(3):
        landing[which][me] = send_ref[which, me]

    def transform(which, spectrum):
        @pl.loop(0, INNER // 2)
        def _(tile):
            columns = pl.ds(pl.multiple_of(tile * 2 * LANES, 2 * LANES), 2 * LANES)
            rows = landing[which][:, :, columns].reshape(blocks, 2 * LANES)
            spectrum[:, columns] = jnp.dot(
                forward_ref[...],
                jnp.concatenate([rows, rows], axis=0),
                preferred_element_type=f32,
            )

    for step in range(1, groups):
        wait_from(0, step)
    transform(0, spec_u)
    for step in range(1, groups):
        wait_from(1, step)
        if step == groups // 2:
            for later in range(1, groups):
                copy_to(2, later).start()
    weight_copy(1).start()
    transform(1, spec_h)

    @pl.loop(0, blocks // 8)
    def _(tile):
        real = pl.ds(pl.multiple_of(tile * 8, 8), 8)
        imag = pl.ds(pl.multiple_of(blocks + tile * 8, 8), 8)
        lanes = [slice(b * LANES, (b + 1) * LANES) for b in range(INNER)]
        ur = [spec_u[real, lane] for lane in lanes]
        ui = [spec_u[imag, lane] for lane in lanes]
        hr = [spec_h[real, lane] for lane in lanes]
        hi = [spec_h[imag, lane] for lane in lanes]
        cos, sin = twist_ref[0, real], twist_ref[1, real]

        def term(degree):
            pairs = [(b, degree - b) for b in range(INNER) if 0 <= degree - b < INNER]
            re = sum(ur[b] * hr[d] - ui[b] * hi[d] for b, d in pairs)
            im = sum(ur[b] * hi[d] + ui[b] * hr[d] for b, d in pairs)
            return re, im

        for b in range(INNER):
            re, im = term(b)
            if b + INNER <= 2 * INNER - 2:
                up_re, up_im = term(b + INNER)
                re = re + up_re * cos - up_im * sin
                im = im + up_re * sin + up_im * cos
            spec_u[real, lanes[b]] = re
            spec_u[imag, lanes[b]] = im

    for step in range(1, groups):
        wait_from(2, step)

    @pl.loop(0, INNER // 2)
    def _(tile):
        columns = pl.ds(pl.multiple_of(tile * 2 * LANES, 2 * LANES), 2 * LANES)
        spectrum = spec_u[:, columns]
        high = spectrum.astype(bf16)
        low = (spectrum - high.astype(f32)).astype(bf16)
        convolved = jnp.dot(
            inverse_ref[...],
            jnp.concatenate([high, low, high], axis=0),
            preferred_element_type=f32,
        )
        mixed = series[:, :, columns].reshape(blocks, 2 * LANES).astype(f32)
        gate = gates[:, :, columns].reshape(blocks, 2 * LANES).astype(f32)
        gated_ref[:, columns] = (gate * (convolved + skip_ref[:, columns] * mixed)).astype(bf16)

    pieces = [(split, index) for split in range(splits) for index in range(4)]
    direct = (
        beyond * 2 + side, beyond * 2 + 1 - side,
        near * 2 + side, near * 2 + 1 - side,
        partner,
    )

    def rows_of(piece, towards):
        split, index = piece
        start = (order[index] * 2 + lax.rem(towards, 2)) * part + split * small
        return pl.ds(pl.multiple_of(start, small), small)

    def piece_to(piece, slot):
        return pltpu.make_async_remote_copy(
            src_ref=gated_ref.at[rows_of(piece, direct[slot])],
            dst_ref=landed.at[piece[0], piece[1], me],
            send_sem=piece_send.at[piece[0], piece[1], slot],
            recv_sem=piece_recv.at[piece[0], piece[1], me],
            device_id={"ctx": direct[slot]},
            device_id_type=MESH,
        )

    def pass_on(piece, source, slot):
        place = landed.at[piece[0], piece[1], source]
        return pltpu.make_async_remote_copy(
            src_ref=place,
            dst_ref=place,
            send_sem=pass_send.at[piece[0], piece[1], slot],
            recv_sem=piece_recv.at[piece[0], piece[1], source],
            device_id={"ctx": mate},
            device_id_type=MESH,
        )

    def launch(piece):
        for slot in range(5):
            piece_to(piece, slot).start()
        landed[piece[0], piece[1], me] = gated_ref[rows_of(piece, me)]

    def forward(piece):
        for slot in range(2):
            copy = pass_on(piece, direct[slot], slot)
            copy.wait_recv()
            copy.start()

    far_plane = lax.rem(near + 2, groups // 2)
    passed = (far_plane * 2 + side, far_plane * 2 + 1 - side)

    def partial(piece):
        for source in direct[2:] + passed:
            pass_on(piece, source, 0).wait_recv()
        for source in range(groups):
            for b in range(INNER):
                operand[b * small : (b + 1) * small, source * LANES : (source + 1) * LANES] = landed[
                    piece[0], piece[1], source, :, b * LANES : (b + 1) * LANES
                ]
        for weight, which in ((own_ref, side), (other_ref, 1 - side)):
            columns = pl.ds(pl.multiple_of(which * half, half), half)
            total[:, columns] = jnp.dot(operand[...], weight[...], preferred_element_type=f32)

    def to_sibling(split, index):
        return pltpu.make_async_remote_copy(
            src_ref=sending.at[split, index],
            dst_ref=chip_in.at[split, index],
            send_sem=chip_send.at[split, index],
            recv_sem=chip_recv.at[split, index],
            device_id={"tp": sibling},
            device_id_type=MESH,
        )

    def to_opposite(split):
        return pltpu.make_async_remote_copy(
            src_ref=far_out.at[split],
            dst_ref=far_in.at[split],
            send_sem=far_send.at[split],
            recv_sem=far_recv.at[split],
            device_id={"tp": opposite},
            device_id_type=MESH,
        )

    def to_owner(split):
        return pltpu.make_async_remote_copy(
            src_ref=final.at[split],
            dst_ref=out_ref.at[split],
            send_sem=last_send.at[split],
            recv_sem=last_recv.at[split],
            device_id={"ctx": to_ctx, "tp": to_tp},
            device_id_type=MESH,
        )

    def keep(split):
        return pltpu.make_async_copy(final.at[split], out_ref.at[split], local_sem.at[split])

    window = 2
    for piece in pieces[:window]:
        launch(piece)
    forward(pieces[0])
    weight_copy(0).wait_recv()
    weight_copy(1).wait_recv()
    for number, piece in enumerate(pieces):
        split, index = piece
        if number + window < len(pieces):
            launch(pieces[number + window])
        if number + 1 < len(pieces):
            forward(pieces[number + 1])
        partial(piece)
        if index < 2:
            sending[split, index] = total[...].astype(bf16)
            to_sibling(split, index).start()
        elif index == 2:
            to_sibling(split, 0).wait_recv()
            far_out[split] = (total[...] + chip_in[split, 0].astype(f32)).astype(bf16)
            to_opposite(split).start()
        else:
            to_sibling(split, 1).wait_recv()
            to_opposite(split).wait_recv()
            final[split] = (
                total[...] + chip_in[split, 1].astype(f32) + far_in[split].astype(f32)
            ).astype(bf16)

            @pl.when(leaves)
            def _():
                to_owner(split).start()

            @pl.when(stays)
            def _():
                keep(split).start()

    for which in range(3):
        for step in range(1, groups):
            copy_to(which, step).wait_send()
    for piece in pieces:
        for slot in range(5):
            piece_to(piece, slot).wait_send()
        for slot in range(2):
            pass_on(piece, direct[slot], slot).wait_send()
    for which in range(2):
        weight_copy(which).wait_send()
    for split in range(splits):
        for index in range(2):
            to_sibling(split, index).wait_send()
        to_opposite(split).wait_send()

        @pl.when(leaves)
        def _():
            to_owner(split).wait()

        @pl.when(stays)
        def _():
            keep(split).wait()


def kernel_path(query_rows, key_rows, value_rows, filters, skip_gain, out_weight):
    row_count, chan_count = key_rows.shape
    groups = lax.axis_size("ctx")
    me = lax.axis_index("ctx")
    part = row_count // INNER
    small = 16
    splits = part // small
    piece = small * INNER
    wide = INNER * LANES
    blocks = groups * part
    depth, half = out_weight.shape
    mixed_in = (key_rows.astype(f32) * value_rows.astype(f32)).astype(bf16)

    def by_group(rows):
        cut = rows.reshape(part, INNER, groups, LANES)
        return cut.transpose(2, 0, 1, 3).reshape(groups, part, wide)

    sent = jnp.stack([by_group(mixed_in), by_group(filters), by_group(query_rows)])
    skip = jnp.tile(lax.dynamic_slice(skip_gain, (me * LANES,), (LANES,)), INNER)[None, :]
    forward, inverse, twist = block_tables(blocks)
    vmem = pl.BlockSpec(memory_space=pltpu.VMEM)
    dma = pltpu.SemaphoreType.DMA
    result = pl.pallas_call(
        functools.partial(mixer_kernel, groups),
        out_shape=jax.ShapeDtypeStruct((splits, piece, 2 * half), bf16),
        in_specs=[vmem] * 6,
        out_specs=pl.BlockSpec(memory_space=pl.ANY),
        scratch_shapes=[
            pltpu.VMEM((groups, part, wide), bf16),
            pltpu.VMEM((groups, part, wide), bf16),
            pltpu.VMEM((groups, part, wide), bf16),
            pltpu.VMEM((2 * blocks, wide), f32),
            pltpu.VMEM((2 * blocks, wide), f32),
            pltpu.VMEM((blocks, wide), bf16),
            pltpu.VMEM((depth, half), bf16),
            pltpu.VMEM((splits, 4, groups, small, wide), bf16),
            pltpu.VMEM((piece, chan_count), bf16),
            pltpu.VMEM((piece, 2 * half), f32),
            pltpu.VMEM((splits, 2, piece, 2 * half), bf16),
            pltpu.VMEM((splits, 2, piece, 2 * half), bf16),
            pltpu.VMEM((splits, piece, 2 * half), bf16),
            pltpu.VMEM((splits, piece, 2 * half), bf16),
            pltpu.VMEM((splits, piece, 2 * half), bf16),
            dma((3, groups)),
            dma((3, groups)),
            dma((2,)),
            dma((2,)),
            dma((splits, 4, 5)),
            dma((splits, 4, groups)),
            dma((splits, 4, 2)),
            dma((splits, 2)),
            dma((splits, 2)),
            dma((splits,)),
            dma((splits,)),
            dma((splits,)),
            dma((splits,)),
            dma((splits,)),
        ],
        compiler_params=pltpu.CompilerParams(
            collective_id=0, has_side_effects=True, vmem_limit_bytes=40 * 2**20
        ),
        name="mixer",
    )(sent, out_weight, skip, jnp.asarray(forward), jnp.asarray(inverse), jnp.asarray(twist))
    result = result.reshape(splits, INNER, small, 2 * half)
    return result.transpose(0, 2, 1, 3).reshape(row_count, 2 * half)


def on_device(query_rows, key_rows, value_rows, filters, skip_gain, out_weight):
    row_count, chan_count = key_rows.shape
    groups, shares = lax.axis_size("ctx"), lax.axis_size("tp")
    fits = (
        shares == 4
        and groups == 2 * shares
        and chan_count == groups * LANES
        and row_count % (16 * INNER) == 0
        and groups * row_count <= 2048
    )
    path = kernel_path if fits else plain_path
    return path(query_rows, key_rows, value_rows, filters, skip_gain, out_weight)


def solution(mesh):
    in_specs = (
        P("ctx", "tp"),
        P("ctx", "tp"),
        P("ctx", "tp"),
        P("ctx", "tp"),
        P("tp"),
        P("tp", "ctx"),
    )
    out_specs = P("ctx", "tp")
    return jax.shard_map(
        on_device, mesh=mesh, in_specs=in_specs, out_specs=out_specs, check_vma=False
    )
```
